32 devices in a mesh: pipe: 2 (over x), seq: 4 (over y, core), fsdp: 4 (over z).
Axes of the slice: x: 2, y: 2, z: 4, core: 2. Of those that a mesh axis runs over, the one named last changes fastest.
Arguments:
- embedded: bfloat16 [512, 2688], P('seq', 'fsdp'), may hold values from -6 to 6
- sent_forward: bfloat16 [2, 512, 2688], P('pipe', 'seq', 'fsdp'), may hold values from -6 to 6
- stashed: bfloat16 [2, 512, 2688], P('pipe', 'seq', 'fsdp'), may hold values from -6 to 6
- sent_backward: bfloat16 [2, 512, 2688], P('pipe', 'seq', 'fsdp'), may hold values from -6 to 6
- loss_grad: bfloat16 [512, 2688], P('seq', 'fsdp'), may hold values from -6 to 6
- norm_gain: float32 [2, 2688], P('pipe'), may hold values from 0.5 to 2
- w_query: bfloat16 [2, 2688, 2048], P('pipe', None, 'fsdp'), may hold values from -1 to 1
- w_key: bfloat16 [2, 2688, 1024], P('pipe', None, 'fsdp'), may hold values from -1 to 1
- value_projection: bfloat16 [2, 2688, 1024], P('pipe', None, 'fsdp'), may hold values from -0.125 to 0.125
- w_out: bfloat16 [2, 2048, 2688], P('pipe', 'fsdp'), may hold values from -0.125 to 0.125
- forward_docs: int32 [2, 512], P('pipe'), may hold values from 0 to 3, never falling along the last dimension, each value on 1 to 256 neighbouring positions
- backward_docs: int32 [2, 512], P('pipe'), may hold values from 0 to 3, never falling along the last dimension, each value on 1 to 256 neighbouring positions
Outputs:
- forward_out: bfloat16 [2, 512, 2688], P('pipe', 'seq', 'fsdp')
- input_grad: bfloat16 [2, 512, 2688], P('pipe', 'seq', 'fsdp')
The draws below stay inside these ranges and needn't reach their ends.
Inputs may be any that keep to these rules, and one draw needn't show every extreme that they name: `forward_docs`: document numbers never fall along a sequence; every document is a run of 1 to 256 tokens. `backward_docs`: document numbers never fall along a sequence; every document is a run of 1 to 256 tokens.
All inputs are finite; a program needn't handle non-finite values.
Results may differ from the reference program's by a relative error of at most 0.015.
Values may be sent and summed in bfloat16 or wider, within the bound.
A program may use at most 64 MiB of HBM per device.

```python
import math
import jax
import jax.numpy as jnp
import numpy as np
from jax import lax

MODEL_WIDTH = 2688
QUERY_HEADS = 16
KEY_VALUE_HEADS = 8
HEAD_SIZE = 128
WINDOW_TOKENS = 512
SHARD_TOKENS = 128
SEQUENCE_TOKENS = 512
N_PIPE = 2
N_SEQ = 4


def plant_pattern(key):
    pattern_random_key = jax.random.fold_in(key, 9173)
    head_sign_flips = (jax.random.randint(jax.random.fold_in(pattern_random_key, 3), (KEY_VALUE_HEADS, HEAD_SIZE), 0, 2) * 2 - 1).astype(jnp.float32)
    return head_sign_flips


def draw_rows(key, leading, salt):
    own_key = jax.random.fold_in(key, salt)
    full_shape = leading + (SEQUENCE_TOKENS, MODEL_WIDTH)
    drawn = jax.random.truncated_normal(own_key, -6.0, 6.0, full_shape, jnp.float32)
    return drawn.astype(jnp.bfloat16)


def draw_projection(key, aligned_rows, salt):
    own_key = jax.random.fold_in(key, salt)
    columns = aligned_rows.shape[0]
    spread = MODEL_WIDTH ** (-0.5)
    full_shape = (N_PIPE, MODEL_WIDTH, columns)
    drawn = jax.random.truncated_normal(own_key, -6.0, 6.0, full_shape, jnp.float32) * spread
    return drawn.astype(jnp.bfloat16)


def draw_embedded(key, part):
    return draw_rows(key, (), 11)


def draw_sent_forward(key, part):
    return draw_rows(key, (N_PIPE,), 12)


def draw_stashed(key, part):
    return draw_rows(key, (N_PIPE,), 13)


def draw_w_query(key, part):
    head_sign_flips = plant_pattern(key)
    aligned_rows = jnp.repeat(head_sign_flips, QUERY_HEADS // KEY_VALUE_HEADS, axis=0).reshape(QUERY_HEADS * HEAD_SIZE)
    return draw_projection(key, aligned_rows, 21)


def draw_w_key(key, part):
    head_sign_flips = plant_pattern(key)
    aligned_rows = head_sign_flips.reshape(KEY_VALUE_HEADS * HEAD_SIZE)
    return draw_projection(key, aligned_rows, 22)


def levels(rng, shape, shards, least, high):
    level = 1.0
    for dim, shards_of in shards:
        draws = jax.random.uniform(jax.random.fold_in(jax.random.fold_in(rng, 6), dim), (shards_of,), jnp.float32, least / len(shards), high / len(shards))
        level = level * jnp.repeat(jnp.exp(draws), shape[dim] // shards_of).reshape((-1,) + (1,) * (len(shape) - 1 - dim))
    return level


def split_up(number_of, total, bound, skew):
    loads = [(1 << 20) // math.isqrt(standing ** skew) + 1 for standing in range(2, number_of + 1)]
    rest, given = total - bound - (number_of - 1), [1] * (number_of - 1)
    while rest > 0:
        free = [i for i in range(number_of - 1) if given[i] < bound]
        whole, budget = sum([loads[i] for i in free]), rest
        for i in free:
            extra = min(bound - given[i], max(1, budget * loads[i] // whole), rest)
            given[i] = given[i] + extra
            rest = rest - extra
    return np.array([bound] + given)


def ragged(key, amount, total, limit, lean):
    if amount == 2:
        one = jax.random.randint(key, (), max(1, total - limit), min(limit, total - 1) + 1)
        return jnp.stack([one, total - one])
    lengths = jnp.asarray(split_up(amount, total, limit, lean), jnp.int32)
    couples = (amount - 1) // 2
    source_of, receiver = lengths[1:1 + 2 * couples:2], lengths[2:2 + 2 * couples:2]
    margin = jnp.minimum(source_of - 1, limit - receiver)
    moved = jax.random.randint(jax.random.fold_in(key, 1), (couples,), 0, 1 << 20) % (margin + 1)
    lengths = lengths.at[1:1 + 2 * couples:2].set(source_of - moved).at[2:2 + 2 * couples:2].set(receiver + moved)
    return lengths[jax.random.permutation(jax.random.fold_in(key, 2), amount)]


def normal_values(key, extent, scale, limit, split=(), held_as=jnp.bfloat16):
    loudness = levels(key, extent, split, -0.22, 0.18) if split else 1.0
    array = jax.random.normal(key, extent, jnp.float32) * scale * loudness
    return jnp.minimum(jnp.maximum(array, -limit), limit).astype(held_as)


def setup_inputs(seed: int = 0) -> dict:
    key_list = jax.random.split(jax.random.key(seed), 13)
    return {
        "embedded": draw_embedded(jax.random.fold_in(key_list[12], 71), 0),
        "sent_forward": draw_sent_forward(jax.random.fold_in(key_list[12], 71), 0),
        "stashed": draw_stashed(jax.random.fold_in(key_list[12], 71), 0),
        "sent_backward": normal_values(key_list[3], (N_PIPE, SEQUENCE_TOKENS, MODEL_WIDTH), 1.0, 6.0, ((0, 2), (1, 4), (2, 4))),
        "loss_grad": normal_values(key_list[4], (SEQUENCE_TOKENS, MODEL_WIDTH), 1.0, 6.0, ((0, 4), (1, 4))),
        "norm_gain": jnp.clip(jnp.exp(math.log(2.0) - 1.3862944 * jax.random.uniform(key_list[5], (N_PIPE, MODEL_WIDTH), jnp.float32) ** levels(key_list[5], (N_PIPE, MODEL_WIDTH), ((0, 2),), -0.2, 0.2)), 0.5, 2.0),
        "w_query": draw_w_query(jax.random.fold_in(key_list[12], 71), 0),
        "w_key": draw_w_key(jax.random.fold_in(key_list[12], 71), 0),
        "value_projection": normal_values(key_list[8], (N_PIPE, MODEL_WIDTH, KEY_VALUE_HEADS * HEAD_SIZE), MODEL_WIDTH ** -0.5, 0.125, ((0, 2), (2, 4))),
        "w_out": normal_values(key_list[9], (N_PIPE, QUERY_HEADS * HEAD_SIZE, MODEL_WIDTH), (QUERY_HEADS * HEAD_SIZE) ** -0.5, 0.125, ((0, 2), (1, 4))),
        "forward_docs": jax.vmap(lambda own: jnp.searchsorted(jnp.cumsum(ragged(own, 4, SEQUENCE_TOKENS, SEQUENCE_TOKENS // 2, 1)), jnp.arange(SEQUENCE_TOKENS), side="right"))(jax.random.split(key_list[10], N_PIPE)).reshape((N_PIPE, SEQUENCE_TOKENS)).astype(jnp.int32),
        "backward_docs": jax.vmap(lambda own: jnp.searchsorted(jnp.cumsum(ragged(own, 4, SEQUENCE_TOKENS, SEQUENCE_TOKENS // 2, 1)), jnp.arange(SEQUENCE_TOKENS), side="right"))(jax.random.split(key_list[11], N_PIPE)).reshape((N_PIPE, SEQUENCE_TOKENS)).astype(jnp.int32),
    }


def normalize(rows_in, gain):
    value_rows = rows_in.astype(jnp.float32)
    row_scale_factor = lax.rsqrt(lax.optimization_barrier(jnp.mean(value_rows * value_rows, axis=-1, keepdims=True)) + 1e-06)
    return ((value_rows * row_scale_factor * gain).astype(jnp.bfloat16), row_scale_factor)

def padded_docs(docs):
    return jnp.concatenate([jnp.full((WINDOW_TOKENS,), -1, jnp.int32), docs.astype(jnp.int32)])

def block_probs(query_block, k_block, q_pos, k_pos, q_doc, k_doc):
    scores = jnp.einsum('qhgd,khd->hgqk', query_block.astype(jnp.float32), k_block.astype(jnp.float32))
    scores = scores * HEAD_SIZE ** (-0.5)
    keep = (k_pos[None, :] <= q_pos[:, None]) & (q_pos[:, None] - k_pos[None, :] < WINDOW_TOKENS)
    keep = keep & (k_doc[None, :] == q_doc[:, None])
    scores = jnp.where(keep, scores, -1e+30)
    top = lax.optimization_barrier(jnp.max(scores, axis=-1, keepdims=True))
    expo = jnp.exp(scores - top)
    return expo / lax.optimization_barrier(jnp.sum(expo, axis=-1, keepdims=True))

def project(x_rows, gain, wq, wk, wv):
    h_rows, row_scale_factor = normalize(x_rows, gain)
    query_rows = jnp.dot(h_rows, wq, preferred_element_type=jnp.float32).astype(jnp.bfloat16)
    key_rows = jnp.dot(h_rows, wk, preferred_element_type=jnp.float32).astype(jnp.bfloat16)
    value_rows = jnp.dot(h_rows, wv, preferred_element_type=jnp.float32).astype(jnp.bfloat16)
    return (query_rows, key_rows.reshape(SEQUENCE_TOKENS, KEY_VALUE_HEADS, HEAD_SIZE), value_rows.reshape(SEQUENCE_TOKENS, KEY_VALUE_HEADS, HEAD_SIZE), row_scale_factor)

def block_inputs(query_rows, key_pad, value_pad, doc_pad, index):
    head_groups = QUERY_HEADS // KEY_VALUE_HEADS
    query_start = (index * SHARD_TOKENS).astype(jnp.int32)
    query_block = lax.dynamic_slice_in_dim(query_rows, query_start, SHARD_TOKENS, 0).reshape(SHARD_TOKENS, KEY_VALUE_HEADS, head_groups, HEAD_SIZE)
    k_block = lax.dynamic_slice_in_dim(key_pad, query_start, WINDOW_TOKENS + SHARD_TOKENS, 0)
    v_block = lax.dynamic_slice_in_dim(value_pad, query_start, WINDOW_TOKENS + SHARD_TOKENS, 0)
    q_pos = query_start + jnp.arange(SHARD_TOKENS, dtype=jnp.int32)
    k_pos = query_start - WINDOW_TOKENS + jnp.arange(WINDOW_TOKENS + SHARD_TOKENS, dtype=jnp.int32)
    q_doc = lax.dynamic_slice_in_dim(doc_pad, query_start + WINDOW_TOKENS, SHARD_TOKENS, 0)
    k_doc = lax.dynamic_slice_in_dim(doc_pad, query_start, WINDOW_TOKENS + SHARD_TOKENS, 0)
    return (query_block, k_block, v_block, q_pos, k_pos, q_doc, k_doc)

def pad_rows(block):
    return jnp.concatenate([jnp.zeros((WINDOW_TOKENS,) + block.shape[1:], block.dtype), block], 0)

def layer_forward(x_rows, gain, wq, wk, wv, wo, docs):
    query_rows, key_rows, value_rows, row_scale_factor = project(x_rows, gain, wq, wk, wv)
    key_pad, value_pad, doc_pad = (pad_rows(key_rows), pad_rows(value_rows), padded_docs(docs))

    def one_block(index):
        query_block, k_block, v_block, q_pos, k_pos, q_doc, k_doc = block_inputs(query_rows, key_pad, value_pad, doc_pad, index)
        probs = block_probs(query_block, k_block, q_pos, k_pos, q_doc, k_doc).astype(jnp.bfloat16)
        attn = jnp.einsum('hgqk,khd->qhgd', probs.astype(jnp.float32), v_block.astype(jnp.float32))
        return attn.reshape(SHARD_TOKENS, QUERY_HEADS * HEAD_SIZE).astype(jnp.bfloat16)
    attn_all = lax.map(one_block, jnp.arange(N_SEQ, dtype=jnp.int32)).reshape(SEQUENCE_TOKENS, QUERY_HEADS * HEAD_SIZE)
    mixed = jnp.dot(attn_all, wo, preferred_element_type=jnp.float32)
    return (x_rows.astype(jnp.float32) + mixed).astype(jnp.bfloat16)

def layer_backward(x_rows, upstream, gain, wq, wk, wv, wo, docs):
    query_rows, key_rows, value_rows, row_scale_factor = project(x_rows, gain, wq, wk, wv)
    key_pad, value_pad, doc_pad = (pad_rows(key_rows), pad_rows(value_rows), padded_docs(docs))
    attention_gradient = jnp.dot(upstream, wo.T, preferred_element_type=jnp.float32).astype(jnp.bfloat16)

    def one_block(carry, index):
        key_gradient_padded, value_gradient_padded = carry
        query_block, k_block, v_block, q_pos, k_pos, q_doc, k_doc = block_inputs(query_rows, key_pad, value_pad, doc_pad, index)
        probs = block_probs(query_block, k_block, q_pos, k_pos, q_doc, k_doc)
        probs_low = probs.astype(jnp.bfloat16).astype(jnp.float32)
        query_start = (index * SHARD_TOKENS).astype(jnp.int32)
        attention_block_gradient = lax.dynamic_slice_in_dim(attention_gradient, query_start, SHARD_TOKENS, 0).reshape(SHARD_TOKENS, KEY_VALUE_HEADS, QUERY_HEADS // KEY_VALUE_HEADS, HEAD_SIZE).astype(jnp.float32)
        dv_block = jnp.einsum('hgqk,qhgd->khd', probs_low, attention_block_gradient)
        dp_block = jnp.einsum('qhgd,khd->hgqk', attention_block_gradient, v_block.astype(jnp.float32))
        delta = lax.optimization_barrier(jnp.sum(probs * dp_block, axis=-1, keepdims=True))
        ds_block = (probs * (dp_block - delta)).astype(jnp.bfloat16).astype(jnp.float32)
        dq_block = jnp.einsum('hgqk,khd->qhgd', ds_block, k_block.astype(jnp.float32)) * HEAD_SIZE ** (-0.5)
        dk_block = jnp.einsum('hgqk,qhgd->khd', ds_block, query_block.astype(jnp.float32)) * HEAD_SIZE ** (-0.5)
        old_k = lax.dynamic_slice_in_dim(key_gradient_padded, query_start, WINDOW_TOKENS + SHARD_TOKENS, 0)
        old_v = lax.dynamic_slice_in_dim(value_gradient_padded, query_start, WINDOW_TOKENS + SHARD_TOKENS, 0)
        key_gradient_padded = lax.dynamic_update_slice_in_dim(key_gradient_padded, old_k + dk_block, query_start, 0)
        value_gradient_padded = lax.dynamic_update_slice_in_dim(value_gradient_padded, old_v + dv_block, query_start, 0)
        return ((key_gradient_padded, value_gradient_padded), dq_block.reshape(SHARD_TOKENS, QUERY_HEADS * HEAD_SIZE).astype(jnp.bfloat16))
    padded_start = jnp.zeros((WINDOW_TOKENS + SEQUENCE_TOKENS, KEY_VALUE_HEADS, HEAD_SIZE), jnp.float32)
    (key_gradient_padded, value_gradient_padded), dq_all = lax.scan(one_block, (padded_start, padded_start), jnp.arange(N_SEQ, dtype=jnp.int32))
    dq_all = dq_all.reshape(SEQUENCE_TOKENS, QUERY_HEADS * HEAD_SIZE)
    key_gradient_total = key_gradient_padded[WINDOW_TOKENS:].reshape(SEQUENCE_TOKENS, KEY_VALUE_HEADS * HEAD_SIZE).astype(jnp.bfloat16)
    value_gradient_total = value_gradient_padded[WINDOW_TOKENS:].reshape(SEQUENCE_TOKENS, KEY_VALUE_HEADS * HEAD_SIZE).astype(jnp.bfloat16)
    d_norm = jnp.dot(dq_all, wq.T, preferred_element_type=jnp.float32)
    d_norm = d_norm + jnp.dot(key_gradient_total, wk.T, preferred_element_type=jnp.float32)
    d_norm = d_norm + jnp.dot(value_gradient_total, wv.T, preferred_element_type=jnp.float32)
    values_in = x_rows.astype(jnp.float32)
    row_mean = lax.optimization_barrier(jnp.mean(values_in * gain * d_norm, axis=-1, keepdims=True))
    d_input = row_scale_factor * gain * d_norm - values_in * row_scale_factor ** 3 * row_mean
    return (upstream.astype(jnp.float32) + d_input).astype(jnp.bfloat16)

def reference(embedded, sent_forward, stashed, sent_backward, loss_grad, norm_gain, w_query, w_key, value_projection, w_out, forward_docs, backward_docs):
    outputs = []
    gradients = []
    for section in range(N_PIPE):
        x_rows = embedded if section == 0 else sent_forward[section - 1]
        upstream = loss_grad if section == N_PIPE - 1 else sent_backward[section + 1]
        outputs.append(layer_forward(x_rows, norm_gain[section], w_query[section], w_key[section], value_projection[section], w_out[section], forward_docs[section]))
        gradients.append(layer_backward(stashed[section], upstream, norm_gain[section], w_query[section], w_key[section], value_projection[section], w_out[section], backward_docs[section]))
    return (jnp.stack(outputs), jnp.stack(gradients))
```

```python
import functools

import jax
import jax.numpy as jnp
from jax import lax
from jax.experimental import pallas as pl
from jax.experimental.pallas import tpu as pltpu
from jax.sharding import PartitionSpec as P

MODEL_WIDTH = 2688
HEAD_SIZE = 128
WINDOW_TOKENS = 512
MESH = pl.DeviceIdType.MESH
F32 = jnp.float32
BF16 = jnp.bfloat16
STASH, UP, ROWS = 0, 1, 2
BWD, FWD = 0, 1


def nn(left, right):
    return lax.dot_general(left, right, (((1,), (0,)), ((), ())), preferred_element_type=F32)


def nt(left, right):
    return lax.dot_general(left, right, (((1,), (1,)), ((), ())), preferred_element_type=F32)


def tn(left, right):
    return lax.dot_general(left, right, (((0,), (0,)), ((), ())), preferred_element_type=F32)


def kernel(
    sizes,
    embedded,
    sent_forward,
    stashed,
    sent_backward,
    loss_grad,
    gain_ref,
    w_query,
    w_key,
    w_value,
    w_out,
    docs_fwd,
    docs_bwd,
    forward_out,
    input_grad,
    wq,
    wk,
    wv,
    wo,
    gathered,
    gain_parts,
    kv_window,
    q_rows,
    probs,
    terms,
    pair_out,
    pair_in,
    chip_out,
    chip_in,
    part,
    rs_out,
    rs_in,
    stat_out,
    stat_in,
    local_sem,
    send_sem,
    gather_sem,
    pipe_sem,
    kv_sem,
    pair_sem,
    chip_sem,
    rs_sem,
    stat_sem,
):
    sections, chips, groups, reach = sizes
    length, share = embedded.shape
    section = lax.axis_index("pipe")
    seq = lax.axis_index("seq")
    z = lax.axis_index("fsdp")
    chip, core = seq // 2, lax.rem(seq, 2)
    sibling = seq + 1 - 2 * core
    slots = 2 * (reach + 1)
    scale = HEAD_SIZE ** (-0.5)
    pending = []

    def when(cond, action):
        pl.when(cond)(action)

    def remote(src, dst, recv, target):
        index = len(pending)
        copy = pltpu.make_async_remote_copy(
            src_ref=src,
            dst_ref=dst,
            send_sem=send_sem.at[index],
            recv_sem=recv,
            device_id=target,
            device_id_type=MESH,
        )
        return copy

    def send(cond, src, dst, recv, target):
        copy = remote(src, dst, recv, target)
        pending.append((cond, copy))
        when(cond, lambda: copy.start())

    def arrive(cond, dst, recv, target):
        copy = pltpu.make_async_remote_copy(
            src_ref=dst,
            dst_ref=dst,
            send_sem=send_sem.at[0],
            recv_sem=recv,
            device_id=target,
            device_id_type=MESH,
        )
        when(cond, lambda: copy.wait_recv())

    def local(src, dst, index):
        return pltpu.make_async_copy(src, dst, local_sem.at[index])

    own_stash = local(stashed.at[0], gathered.at[STASH, z], 0)
    own_up = local(loss_grad, gathered.at[UP, z], 1)
    own_rows = local(embedded, gathered.at[ROWS, z], 2)
    weights = [
        local(w_key.at[0], wk, 3),
        local(w_value.at[0], wv, 4),
        local(w_query.at[0], wq, 5),
        local(w_out.at[0], wo, 6),
    ]
    own_stash.start()
    when(section == sections - 1, lambda: own_up.start())
    when(section == 0, lambda: own_rows.start())
    for copy in weights:
        copy.start()

    barrier = pltpu.get_barrier_semaphore()
    neighbours = [
        (z > 0, {"fsdp": z - 1}),
        (z < groups - 1, {"fsdp": z + 1}),
        (section > 0, {"pipe": section - 1}),
        (section < sections - 1, {"pipe": section + 1}),
        (seq >= 0, {"seq": sibling}),
    ]
    for e in range(1, reach + 1):
        neighbours.append((chip >= e, {"seq": seq - 2 * e}))
        neighbours.append((chip + e < chips, {"seq": seq + 2 * e}))
    for d in range(2, groups):
        neighbours.append((z - d >= 0, {"fsdp": z - d}))
        neighbours.append((z + d < groups, {"fsdp": z + d}))
    total = jnp.int32(0)
    for cond, target in neighbours:
        total = total + cond.astype(jnp.int32)

        def greet(target=target):
            pl.semaphore_signal(barrier, inc=1, device_id=target, device_id_type=MESH)

        when(cond, greet)
    pl.semaphore_wait(barrier, total)

    send(
        section > 0,
        sent_backward.at[0],
        gathered.at[UP, z],
        pipe_sem.at[0],
        {"pipe": section - 1},
    )
    send(
        section < sections - 1,
        sent_forward.at[0],
        gathered.at[ROWS, z],
        pipe_sem.at[1],
        {"pipe": section + 1},
    )

    def gather_from(array, distance):
        low, high = z - distance, z + distance
        if distance:
            arrive(low >= 0, gathered.at[array, low], gather_sem.at[array, low], {"fsdp": z - 1})
        send(
            (low >= 0) & (z < groups - 1),
            gathered.at[array, low],
            gathered.at[array, low],
            gather_sem.at[array, low],
            {"fsdp": z + 1},
        )
        if distance:
            arrive(
                high < groups, gathered.at[array, high], gather_sem.at[array, high], {"fsdp": z + 1}
            )
        send(
            (high < groups) & (z > 0),
            gathered.at[array, high],
            gathered.at[array, high],
            gather_sem.at[array, high],
            {"fsdp": z - 1},
        )

    def whole_rows(array):
        return jnp.concatenate([gathered[array, j] for j in range(groups)], axis=1)

    gain = gain_ref[...]

    def project(array, which):
        rows = whole_rows(array).astype(F32)
        row_scale = lax.rsqrt(jnp.mean(rows * rows, axis=-1, keepdims=True) + 1e-06)
        h = (rows * row_scale * gain).astype(BF16)
        half = wk.shape[1]
        kv_window[which, core, :, :half] = nn(h, wk[...]).astype(BF16)
        kv_window[which, core, :, half:] = nn(h, wv[...]).astype(BF16)
        spread(which)
        q_rows[which] = nn(h, wq[...]).astype(BF16)
        return row_scale

    def spread(which):
        for e in range(1, reach + 1):
            slot = 2 * e + core
            send(
                chip + e < chips,
                kv_window.at[which, core],
                kv_window.at[which, slot],
                kv_sem.at[which, slot],
                {"seq": seq + 2 * e},
            )
        send(
            core == 0,
            kv_window.at[which, core],
            kv_window.at[which, core],
            kv_sem.at[which, core],
            {"seq": sibling},
        )

    def share_pair(which):
        for e in range(1, reach + 1):
            slot = 2 * e + core
            arrive(
                chip >= e, kv_window.at[which, slot], kv_sem.at[which, slot], {"seq": sibling}
            )
            send(
                chip >= e,
                kv_window.at[which, slot],
                kv_window.at[which, slot],
                kv_sem.at[which, slot],
                {"seq": sibling},
            )

    def take_pair(which):
        arrive(core == 1, kv_window.at[which, 0], kv_sem.at[which, 0], {"seq": sibling})
        for e in range(1, reach + 1):
            slot = 2 * e + 1 - core
            arrive(
                chip >= e, kv_window.at[which, slot], kv_sem.at[which, slot], {"seq": sibling}
            )

    def clear_absent():
        for which in (BWD, FWD):

            def clear(slot, which=which):
                kv_window[which, slot] = jnp.zeros(kv_window.shape[2:], BF16)

            when(core == 0, lambda: clear(1))
            for e in range(1, reach + 1):

                def both(e=e):
                    clear(2 * e)
                    clear(2 * e + 1)

                when(chip < e, both)

    def keep_mask(docs):
        start = pl.multiple_of(seq * length, 128)
        own = docs[:, pl.ds(start, length)].astype(F32)
        own_docs = jnp.transpose(jnp.broadcast_to(own, (length, length)))
        q_pos = seq * length + lax.broadcasted_iota(jnp.int32, (length, length), 0)
        pieces = []
        for slot in range(slots):
            first = (2 * (chip - slot // 2) + slot % 2) * length
            at = pl.multiple_of(jnp.maximum(first, 0), 128)
            other = docs[:, pl.ds(at, length)].astype(F32)
            k_pos = first + lax.broadcasted_iota(jnp.int32, (length, length), 1)
            keep = (k_pos >= 0) & (k_pos <= q_pos) & (q_pos - k_pos < WINDOW_TOKENS)
            keep = keep & (own_docs == jnp.broadcast_to(other, (length, length)))
            pieces.append(jnp.where(keep, 0.0, -1e30))
        bias = jnp.concatenate(pieces, axis=1)
        return jnp.concatenate([bias, bias], axis=0)

    def window_part(which, column):
        return jnp.concatenate(
            [
                kv_window[which, slot, :, column * HEAD_SIZE : (column + 1) * HEAD_SIZE]
                for slot in range(slots)
            ],
            axis=0,
        )

    def pair_rows(values, head):
        low = 2 * head * HEAD_SIZE
        return jnp.concatenate(
            [values[:, low : low + HEAD_SIZE], values[:, low + HEAD_SIZE : low + 2 * HEAD_SIZE]],
            axis=0,
        )

    kv_heads = wk.shape[1] // HEAD_SIZE

    def softmax(which, head, bias):
        queries = pair_rows(q_rows[which], head)
        scores = nt(queries, window_part(which, head)) * scale
        scores = jnp.where(bias < 0.0, bias, scores)
        top = jnp.max(scores, axis=-1, keepdims=True)
        expo = jnp.exp(scores - top)
        return expo / jnp.sum(expo, axis=-1, keepdims=True)

    def scatter_from(which, distance):
        high, low = z + distance, z - distance
        for side, at, cond, more, target in (
            (0, high, high < groups, z > 0, {"fsdp": z + 1}),
            (1, low, low >= 0, z < groups - 1, {"fsdp": z - 1}),
        ):

            arrive(cond & more, rs_in.at[which, side, at], rs_sem.at[which, side, at], target)

            def added(side=side, at=at):
                rs_out[which, side, at] = (
                    part[which, at] + rs_in[which, side, at].astype(F32)
                ).astype(BF16)

            def alone(side=side, at=at):
                rs_out[which, side, at] = part[which, at].astype(BF16)

            when(cond & more, added)
            when(cond & jnp.logical_not(more), alone)
            send(
                cond,
                rs_out.at[which, side, at],
                rs_in.at[which, side, at],
                rs_sem.at[which, side, at],
                target,
            )

    def scatter_total(which):
        for side, more, source in (
            (0, z > 0, {"fsdp": z - 1}),
            (1, z < groups - 1, {"fsdp": z + 1}),
        ):
            arrive(more, rs_in.at[which, side, z], rs_sem.at[which, side, z], source)

            def add(side=side):
                part[which, z] = part[which, z] + rs_in[which, side, z].astype(F32)

            when(more, add)
        return part[which, z]

    def split_part(which, values):
        for j in range(groups):
            part[which, j] = values[:, j * share : (j + 1) * share]

    own_stash.wait()
    gather_from(STASH, 0)
    when(section == sections - 1, lambda: own_up.wait())
    arrive(section < sections - 1, gathered.at[UP, z], pipe_sem.at[0], {"pipe": section})
    gather_from(UP, 0)
    clear_absent()
    for j in range(groups):
        gain_parts[j] = gain[:, j * share : (j + 1) * share]
    for d in range(1, groups):
        gather_from(STASH, d)
    gather_from(UP, 1)
    when(section == 0, lambda: own_rows.wait())
    arrive(section > 0, gathered.at[ROWS, z], pipe_sem.at[1], {"pipe": section})
    gather_from(ROWS, 0)
    for copy in weights[:3]:
        copy.wait()

    scale_backward = project(STASH, BWD)
    gather_from(UP, 2) if groups > 2 else None
    share_pair(BWD)
    bias = keep_mask(docs_bwd)
    take_pair(BWD)
    for head in range(kv_heads):
        probs[head] = softmax(BWD, head, bias)
    for d in range(3, groups):
        gather_from(UP, d)
    gather_from(ROWS, 1)
    weights[3].wait()
    d_attn = nt(whole_rows(UP), wo[...]).astype(BF16)
    dq_parts = []
    for head in range(kv_heads):
        p = probs[head]
        gradient = pair_rows(d_attn, head)
        keys = window_part(BWD, head)
        dp = nt(gradient, window_part(BWD, kv_heads + head))
        delta = jnp.sum(p * dp, axis=-1, keepdims=True)
        ds = (p * (dp - delta)).astype(BF16)
        dk = tn(ds, pair_rows(q_rows[BWD], head)) * scale
        dv = tn(p.astype(BF16), gradient)
        for slot in range(slots):
            low = head * HEAD_SIZE
            rows = slice(slot * length, (slot + 1) * length)
            terms[slot, :, low : low + HEAD_SIZE] = dk[rows]
            low = low + kv_heads * HEAD_SIZE
            terms[slot, :, low : low + HEAD_SIZE] = dv[rows]
        dq = (nn(ds, keys) * scale).astype(BF16)
        dq_parts += [dq[:length], dq[length:]]
    for e in list(range(1, reach + 1)) + [0]:
        cond = (chip >= e) if e else (core == 1)

        def stage(e=e):
            pair_out[e] = terms[2 * e + 1 - core].astype(BF16)

        when(cond, stage)
        send(cond, pair_out.at[e], pair_in.at[e], pair_sem.at[e], {"seq": sibling})
    for e in range(1, reach + 1):
        arrive(chip >= e, pair_in.at[e], pair_sem.at[e], {"seq": sibling})

        def stage(e=e):
            chip_out[e - 1] = (terms[2 * e + core] + pair_in[e].astype(F32)).astype(BF16)

        when(chip >= e, stage)
        send(
            chip >= e,
            chip_out.at[e - 1],
            chip_in.at[e - 1],
            chip_sem.at[e - 1],
            {"seq": seq - 2 * e},
        )
    gather_from(ROWS, 2) if groups > 2 else None
    dq_local = jnp.concatenate(dq_parts, axis=1)
    d_norm = nt(dq_local, wq[...])
    arrive(core == 0, pair_in.at[0], pair_sem.at[0], {"seq": sibling})

    def add_pair():
        terms[core] = terms[core] + pair_in[0].astype(F32)

    when(core == 0, add_pair)
    for e in range(1, reach + 1):
        arrive(chip + e < chips, chip_in.at[e - 1], chip_sem.at[e - 1], {"seq": sibling})

        def add_chip(e=e):
            terms[core] = terms[core] + chip_in[e - 1].astype(F32)

        when(chip + e < chips, add_chip)
    owned = terms[core].astype(BF16)
    half = wk.shape[1]
    d_norm = d_norm + nt(owned[:, :half], wk[...]) + nt(owned[:, half:], wv[...])
    split_part(BWD, d_norm)
    for d in range(groups - 1, 0, -1):
        if d == 1:
            for far in range(3, groups):
                gather_from(ROWS, far)
        scatter_from(BWD, d)
    rows = whole_rows(STASH).astype(F32)
    row_part = jnp.sum(rows * gain * d_norm, axis=-1, keepdims=True)
    stat_out[...] = jnp.transpose(jnp.broadcast_to(row_part, (length, length)))[:8]
    for d in range(1, groups):
        for cond, other in ((z + d < groups, z + d), (z - d >= 0, z - d)):
            send(cond, stat_out, stat_in.at[z], stat_sem.at[z], {"fsdp": other})

    project(ROWS, FWD)
    share_pair(FWD)
    bias = keep_mask(docs_fwd)
    take_pair(FWD)
    attn_parts = []
    for head in range(kv_heads):
        p = softmax(FWD, head, bias).astype(BF16)
        attn = nn(p, window_part(FWD, kv_heads + head)).astype(BF16)
        attn_parts += [attn[:length], attn[length:]]
    split_part(FWD, nn(jnp.concatenate(attn_parts, axis=1), wo[...]))
    for d in range(groups - 1, 0, -1):
        scatter_from(FWD, d)

    d_share = scatter_total(BWD)
    stat_in[z] = stat_out[...]
    for d in range(1, groups):
        for cond, other in ((z + d < groups, z + d), (z - d >= 0, z - d)):
            arrive(cond, stat_in.at[other], stat_sem.at[other], {"fsdp": other})
    stat = stat_in[0]
    for j in range(1, groups):
        stat = stat + stat_in[j]
    stat = jnp.broadcast_to(stat[:1], (length, length))
    row_mean = jnp.transpose(stat)[:, :1] / MODEL_WIDTH
    own = gathered[STASH, z].astype(F32)
    d_input = scale_backward * gain_parts[z] * d_share - own * scale_backward**3 * row_mean
    input_grad[0] = (gathered[UP, z].astype(F32) + d_input).astype(BF16)
    summed = scatter_total(FWD)
    forward_out[0] = (gathered[ROWS, z].astype(F32) + summed).astype(BF16)
    for cond, copy in pending:
        when(cond, lambda copy=copy: copy.wait_send())


def per_device(*args):
    embedded = args[0]
    length, share = embedded.shape
    w_query, w_key, w_out = args[6], args[7], args[9]
    sections = lax.axis_size("pipe")
    chips = lax.axis_size("seq") // 2
    groups = lax.axis_size("fsdp")
    hops = min(WINDOW_TOKENS // length, lax.axis_size("seq") - 1)
    reach = min((hops + 1) // 2, chips - 1)
    slots = 2 * (reach + 1)
    width = w_key.shape[2]
    kv_heads = width // HEAD_SIZE
    anywhere = pl.BlockSpec(memory_space=pl.ANY)
    inside = pl.BlockSpec(memory_space=pltpu.VMEM)
    sent = jax.ShapeDtypeStruct((1, length, share), BF16)
    dma = pltpu.SemaphoreType.DMA
    call = pl.pallas_call(
        functools.partial(kernel, (sections, chips, groups, reach)),
        out_shape=(sent, sent),
        in_specs=[anywhere] * 5 + [inside] + [anywhere] * 4 + [inside] * 2,
        out_specs=(inside, inside),
        scratch_shapes=[
            pltpu.VMEM(w_query.shape[1:], BF16),
            pltpu.VMEM(w_key.shape[1:], BF16),
            pltpu.VMEM(w_key.shape[1:], BF16),
            pltpu.VMEM(w_out.shape[1:], BF16),
            pltpu.VMEM((3, groups, length, share), BF16),
            pltpu.VMEM((groups, 1, share), F32),
            pltpu.VMEM((2, slots, length, 2 * width), BF16),
            pltpu.VMEM((2, length, w_query.shape[2]), BF16),
            pltpu.VMEM((kv_heads, 2 * length, slots * length), F32),
            pltpu.VMEM((slots, length, 2 * width), F32),
            pltpu.VMEM((reach + 1, length, 2 * width), BF16),
            pltpu.VMEM((reach + 1, length, 2 * width), BF16),
            pltpu.VMEM((max(reach, 1), length, 2 * width), BF16),
            pltpu.VMEM((max(reach, 1), length, 2 * width), BF16),
            pltpu.VMEM((2, groups, length, share), F32),
            pltpu.VMEM((2, 2, groups, length, share), BF16),
            pltpu.VMEM((2, 2, groups, length, share), BF16),
            pltpu.VMEM((8, length), F32),
            pltpu.VMEM((groups, 8, length), F32),
            dma((7,)),
            dma((20 * groups + 12 * (reach + 1),)),
            dma((3, groups)),
            dma((2,)),
            dma((2, slots)),
            dma((reach + 1,)),
            dma((max(reach, 1),)),
            dma((2, 2, groups)),
            dma((groups,)),
        ],
        compiler_params=pltpu.CompilerParams(
            collective_id=0, has_side_effects=True, vmem_limit_bytes=56 * 1024 * 1024
        ),
        cost_estimate=pl.CostEstimate(
            flops=4_000_000_000, bytes_accessed=10_000_000, transcendentals=500_000
        ),
    )
    return call(*args)


def solution(mesh):
    placed = (
        P("seq", "fsdp"),
        P("pipe", "seq", "fsdp"),
        P("pipe", "seq", "fsdp"),
        P("pipe", "seq", "fsdp"),
        P("seq", "fsdp"),
        P("pipe", None),
        P("pipe", None, "fsdp"),
        P("pipe", None, "fsdp"),
        P("pipe", None, "fsdp"),
        P("pipe", "fsdp", None),
        P("pipe", None),
        P("pipe", None),
    )
    return jax.shard_map(
        per_device,
        mesh=mesh,
        in_specs=placed,
        out_specs=(P("pipe", "seq", "fsdp"), P("pipe", "seq", "fsdp")),
        check_vma=False,
    )
```

```python
import functools

import jax
import jax.numpy as jnp
from jax import lax
from jax.experimental import pallas as pl
from jax.experimental.pallas import tpu as pltpu
from jax.sharding import PartitionSpec as P

MODEL_WIDTH = 2688
HEAD_SIZE = 128
WINDOW_TOKENS = 512
MESH = pl.DeviceIdType.MESH
F32 = jnp.float32
BF16 = jnp.bfloat16
STASH, UP, ROWS = 0, 1, 2
BWD, FWD = 0, 1


def nn(left, right):
    return lax.dot_general(left, right, (((1,), (0,)), ((), ())), preferred_element_type=F32)


def nt(left, right):
    return lax.dot_general(left, right, (((1,), (1,)), ((), ())), preferred_element_type=F32)


def tn(left, right):
    return lax.dot_general(left, right, (((0,), (0,)), ((), ())), preferred_element_type=F32)


def kernel(
    sizes,
    embedded,
    sent_forward,
    stashed,
    sent_backward,
    loss_grad,
    gain_ref,
    w_query,
    w_key,
    w_value,
    w_out,
    docs_fwd,
    docs_bwd,
    forward_out,
    input_grad,
    wq,
    wk,
    wv,
    wo,
    gathered,
    gain_columns,
    kv_window,
    q_rows,
    probs,
    terms,
    pair_out,
    pair_in,
    chip_out,
    chip_in,
    part,
    rs_out,
    rs_in,
    stat_out,
    stat_in,
    local_sem,
    send_sem,
    gather_sem,
    pipe_sem,
    kv_sem,
    pair_sem,
    chip_sem,
    rs_sem,
    stat_sem,
):
    sections, chips, groups, reach = sizes
    share, length = embedded.shape
    section = lax.axis_index("pipe")
    seq = lax.axis_index("seq")
    z = lax.axis_index("fsdp")
    chip, core = seq // 2, lax.rem(seq, 2)
    sibling = seq + 1 - 2 * core
    slots = 2 * (reach + 1)
    scale = HEAD_SIZE ** (-0.5)
    pending = []

    def when(cond, action):
        pl.when(cond)(action)

    def remote(src, dst, recv, target):
        index = len(pending)
        copy = pltpu.make_async_remote_copy(
            src_ref=src,
            dst_ref=dst,
            send_sem=send_sem.at[index],
            recv_sem=recv,
            device_id=target,
            device_id_type=MESH,
        )
        return copy

    def send(cond, src, dst, recv, target):
        copy = remote(src, dst, recv, target)
        pending.append((cond, copy))
        when(cond, lambda: copy.start())

    def arrive(cond, dst, recv, target):
        copy = pltpu.make_async_remote_copy(
            src_ref=dst,
            dst_ref=dst,
            send_sem=send_sem.at[0],
            recv_sem=recv,
            device_id=target,
            device_id_type=MESH,
        )
        when(cond, lambda: copy.wait_recv())

    def local(src, dst, index):
        return pltpu.make_async_copy(src, dst, local_sem.at[index])

    own_stash = local(stashed.at[0], gathered.at[STASH, z], 0)
    own_up = local(loss_grad, gathered.at[UP, z], 1)
    own_rows = local(embedded, gathered.at[ROWS, z], 2)
    weights = [
        local(w_key.at[0], wk, 3),
        local(w_value.at[0], wv, 4),
        local(w_query.at[0], wq, 5),
        local(w_out.at[0], wo, 6),
    ]
    own_stash.start()
    when(section == sections - 1, lambda: own_up.start())
    when(section == 0, lambda: own_rows.start())
    for copy in weights:
        copy.start()

    barrier = pltpu.get_barrier_semaphore()
    neighbours = [
        (z > 0, {"fsdp": z - 1}),
        (z < groups - 1, {"fsdp": z + 1}),
        (section > 0, {"pipe": section - 1}),
        (section < sections - 1, {"pipe": section + 1}),
        (seq >= 0, {"seq": sibling}),
    ]
    for e in range(1, reach + 1):
        neighbours.append((chip >= e, {"seq": seq - 2 * e}))
        neighbours.append((chip + e < chips, {"seq": seq + 2 * e}))
    for d in range(2, groups):
        neighbours.append((z - d >= 0, {"fsdp": z - d}))
        neighbours.append((z + d < groups, {"fsdp": z + d}))
    total = jnp.int32(0)
    for cond, target in neighbours:
        total = total + cond.astype(jnp.int32)

        def greet(target=target):
            pl.semaphore_signal(barrier, inc=1, device_id=target, device_id_type=MESH)

        when(cond, greet)
    pl.semaphore_wait(barrier, total)

    send(
        section > 0,
        sent_backward.at[0],
        gathered.at[UP, z],
        pipe_sem.at[0],
        {"pipe": section - 1},
    )
    send(
        section < sections - 1,
        sent_forward.at[0],
        gathered.at[ROWS, z],
        pipe_sem.at[1],
        {"pipe": section + 1},
    )

    def gather_from(array, distance, source=None):
        low, high = z - distance, z + distance
        if distance:
            arrive(low >= 0, gathered.at[array, low], gather_sem.at[array, low], {"fsdp": z - 1})
        send(
            (low >= 0) & (z < groups - 1),
            gathered.at[array, low] if source is None else source,
            gathered.at[array, low],
            gather_sem.at[array, low],
            {"fsdp": z + 1},
        )
        if distance:
            arrive(
                high < groups, gathered.at[array, high], gather_sem.at[array, high], {"fsdp": z + 1}
            )
        send(
            (high < groups) & (z > 0),
            gathered.at[array, high] if source is None else source,
            gathered.at[array, high],
            gather_sem.at[array, high],
            {"fsdp": z - 1},
        )

    def whole_rows(array):
        return gathered[array].reshape(groups * share, length)


    def project(array, which):
        rows = whole_rows(array).astype(F32)
        row_scale = lax.rsqrt(jnp.mean(rows * rows, axis=0, keepdims=True) + 1e-06)
        h = jnp.transpose((rows * row_scale * gain_columns[...]).astype(BF16))
        half = wk.shape[1]
        kv_window[which, core, :, :half] = nn(h, wk[...]).astype(BF16)
        kv_window[which, core, :, half:] = nn(h, wv[...]).astype(BF16)
        spread(which)
        q_rows[which] = nn(h, wq[...]).astype(BF16)
        return row_scale

    def spread(which):
        for e in range(1, reach + 1):
            slot = 2 * e + core
            send(
                chip + e < chips,
                kv_window.at[which, core],
                kv_window.at[which, slot],
                kv_sem.at[which, slot],
                {"seq": seq + 2 * e},
            )
        send(
            core == 0,
            kv_window.at[which, core],
            kv_window.at[which, core],
            kv_sem.at[which, core],
            {"seq": sibling},
        )

    def share_pair(which):
        for e in range(1, reach + 1):
            slot = 2 * e + core
            arrive(
                chip >= e, kv_window.at[which, slot], kv_sem.at[which, slot], {"seq": sibling}
            )
            send(
                chip >= e,
                kv_window.at[which, slot],
                kv_window.at[which, slot],
                kv_sem.at[which, slot],
                {"seq": sibling},
            )

    def take_pair(which):
        arrive(core == 1, kv_window.at[which, 0], kv_sem.at[which, 0], {"seq": sibling})
        for e in range(1, reach + 1):
            slot = 2 * e + 1 - core
            arrive(
                chip >= e, kv_window.at[which, slot], kv_sem.at[which, slot], {"seq": sibling}
            )

    def clear_absent():
        for which in (BWD, FWD):

            def clear(slot, which=which):
                kv_window[which, slot] = jnp.zeros(kv_window.shape[2:], BF16)

            when(core == 0, lambda: clear(1))
            for e in range(1, reach + 1):

                def both(e=e):
                    clear(2 * e)
                    clear(2 * e + 1)

                when(chip < e, both)

    def keep_mask(docs):
        start = pl.multiple_of(seq * length, 128)
        own = docs[:, pl.ds(start, length)].astype(F32)
        own_docs = jnp.transpose(jnp.broadcast_to(own, (length, length)))
        q_pos = seq * length + lax.broadcasted_iota(jnp.int32, (length, length), 0)
        pieces = []
        for slot in range(slots):
            first = (2 * (chip - slot // 2) + slot % 2) * length
            at = pl.multiple_of(jnp.maximum(first, 0), 128)
            other = docs[:, pl.ds(at, length)].astype(F32)
            k_pos = first + lax.broadcasted_iota(jnp.int32, (length, length), 1)
            keep = (k_pos >= 0) & (k_pos <= q_pos) & (q_pos - k_pos < WINDOW_TOKENS)
            keep = keep & (own_docs == jnp.broadcast_to(other, (length, length)))
            pieces.append(jnp.where(keep, 0.0, -1e30))
        bias = jnp.concatenate(pieces, axis=1)
        return jnp.concatenate([bias, bias], axis=0)

    def window_part(which, column):
        return jnp.concatenate(
            [
                kv_window[which, slot, :, column * HEAD_SIZE : (column + 1) * HEAD_SIZE]
                for slot in range(slots)
            ],
            axis=0,
        )

    def pair_rows(values, head):
        low = 2 * head * HEAD_SIZE
        return jnp.concatenate(
            [values[:, low : low + HEAD_SIZE], values[:, low + HEAD_SIZE : low + 2 * HEAD_SIZE]],
            axis=0,
        )

    kv_heads = wk.shape[1] // HEAD_SIZE

    def softmax(which, head, bias):
        queries = pair_rows(q_rows[which], head)
        scores = nt(queries, window_part(which, head)) * scale
        scores = jnp.where(bias < 0.0, bias, scores)
        top = jnp.max(scores, axis=-1, keepdims=True)
        expo = jnp.exp(scores - top)
        return expo / jnp.sum(expo, axis=-1, keepdims=True)

    def scatter_from(which, distance):
        high, low = z + distance, z - distance
        for side, at, cond, more, target in (
            (0, high, high < groups, z > 0, {"fsdp": z + 1}),
            (1, low, low >= 0, z < groups - 1, {"fsdp": z - 1}),
        ):

            arrive(cond & more, rs_in.at[which, side, at], rs_sem.at[which, side, at], target)

            def added(side=side, at=at):
                rs_out[which, side, at] = (
                    part[which, at] + rs_in[which, side, at].astype(F32)
                ).astype(BF16)

            def alone(side=side, at=at):
                rs_out[which, side, at] = part[which, at].astype(BF16)

            when(cond & more, added)
            when(cond & jnp.logical_not(more), alone)
            send(
                cond,
                rs_out.at[which, side, at],
                rs_in.at[which, side, at],
                rs_sem.at[which, side, at],
                target,
            )

    def scatter_total(which):
        for side, more, source in (
            (0, z > 0, {"fsdp": z - 1}),
            (1, z < groups - 1, {"fsdp": z + 1}),
        ):
            arrive(more, rs_in.at[which, side, z], rs_sem.at[which, side, z], source)

            def add(side=side):
                part[which, z] = part[which, z] + rs_in[which, side, z].astype(F32)

            when(more, add)
        return part[which, z]

    def split_part(which, values):
        part[which] = values.reshape(groups, share, length)

    gather_from(STASH, 0, stashed.at[0])
    when(section == sections - 1, lambda: own_up.wait())
    arrive(section < sections - 1, gathered.at[UP, z], pipe_sem.at[0], {"pipe": section})
    gather_from(UP, 0)
    clear_absent()
    for low in range(0, groups * share, length):
        row = jnp.broadcast_to(gain_ref[:, low : low + length], (length, length))
        gain_columns[low : low + length] = jnp.transpose(row)
    own_stash.wait()
    for d in range(1, groups):
        gather_from(STASH, d)
    gather_from(UP, 1)
    when(section == 0, lambda: own_rows.wait())
    arrive(section > 0, gathered.at[ROWS, z], pipe_sem.at[1], {"pipe": section})
    gather_from(ROWS, 0)
    for copy in weights[:3]:
        copy.wait()

    scale_backward = project(STASH, BWD)
    gather_from(UP, 2) if groups > 2 else None
    share_pair(BWD)
    bias = keep_mask(docs_bwd)
    take_pair(BWD)
    for head in range(kv_heads):
        probs[head] = softmax(BWD, head, bias)
    for d in range(3, groups):
        gather_from(UP, d)
    gather_from(ROWS, 1)
    weights[3].wait()
    d_attn = jnp.transpose(nn(wo[...], whole_rows(UP)).astype(BF16))
    dq_parts = []
    for head in range(kv_heads):
        p = probs[head]
        gradient = pair_rows(d_attn, head)
        keys = window_part(BWD, head)
        dp = nt(gradient, window_part(BWD, kv_heads + head))
        delta = jnp.sum(p * dp, axis=-1, keepdims=True)
        ds = (p * (dp - delta)).astype(BF16)
        dk = tn(ds, pair_rows(q_rows[BWD], head)) * scale
        dv = tn(p.astype(BF16), gradient)
        for slot in range(slots):
            low = head * HEAD_SIZE
            rows = slice(slot * length, (slot + 1) * length)
            terms[slot, :, low : low + HEAD_SIZE] = dk[rows]
            low = low + kv_heads * HEAD_SIZE
            terms[slot, :, low : low + HEAD_SIZE] = dv[rows]
        dq = (nn(ds, keys) * scale).astype(BF16)
        dq_parts += [dq[:length], dq[length:]]
    for e in list(range(1, reach + 1)) + [0]:
        cond = (chip >= e) if e else (core == 1)

        def stage(e=e):
            pair_out[e] = terms[2 * e + 1 - core].astype(BF16)

        when(cond, stage)
        send(cond, pair_out.at[e], pair_in.at[e], pair_sem.at[e], {"seq": sibling})
    for e in range(1, reach + 1):
        arrive(chip >= e, pair_in.at[e], pair_sem.at[e], {"seq": sibling})

        def stage(e=e):
            chip_out[e - 1] = (terms[2 * e + core] + pair_in[e].astype(F32)).astype(BF16)

        when(chip >= e, stage)
        send(
            chip >= e,
            chip_out.at[e - 1],
            chip_in.at[e - 1],
            chip_sem.at[e - 1],
            {"seq": seq - 2 * e},
        )
    gather_from(ROWS, 2) if groups > 2 else None
    dq_local = jnp.concatenate(dq_parts, axis=1)
    d_norm = nt(wq[...], dq_local)
    arrive(core == 0, pair_in.at[0], pair_sem.at[0], {"seq": sibling})

    def add_pair():
        terms[core] = terms[core] + pair_in[0].astype(F32)

    when(core == 0, add_pair)
    for e in range(1, reach + 1):
        arrive(chip + e < chips, chip_in.at[e - 1], chip_sem.at[e - 1], {"seq": sibling})

        def add_chip(e=e):
            terms[core] = terms[core] + chip_in[e - 1].astype(F32)

        when(chip + e < chips, add_chip)
    owned = terms[core].astype(BF16)
    half = wk.shape[1]
    d_norm = d_norm + nt(wk[...], owned[:, :half]) + nt(wv[...], owned[:, half:])
    split_part(BWD, d_norm)
    for d in range(groups - 1, 0, -1):
        if d == 1:
            for far in range(3, groups):
                gather_from(ROWS, far)
        scatter_from(BWD, d)
    rows = whole_rows(STASH).astype(F32)
    row_part = jnp.sum(rows * gain_columns[...] * d_norm, axis=0, keepdims=True)
    stat_out[...] = jnp.broadcast_to(row_part, (8, length))
    for d in range(1, groups):
        for cond, other in ((z + d < groups, z + d), (z - d >= 0, z - d)):
            send(cond, stat_out, stat_in.at[z], stat_sem.at[z], {"fsdp": other})

    project(ROWS, FWD)
    share_pair(FWD)
    bias = keep_mask(docs_fwd)
    take_pair(FWD)
    attn_parts = []
    for head in range(kv_heads):
        p = softmax(FWD, head, bias).astype(BF16)
        attn = nn(p, window_part(FWD, kv_heads + head)).astype(BF16)
        attn_parts += [attn[:length], attn[length:]]
    split_part(FWD, jnp.transpose(nn(jnp.concatenate(attn_parts, axis=1), wo[...])))
    for d in range(groups - 1, 0, -1):
        scatter_from(FWD, d)

    d_share = scatter_total(BWD)
    stat_in[z] = stat_out[...]
    for d in range(1, groups):
        for cond, other in ((z + d < groups, z + d), (z - d >= 0, z - d)):
            arrive(cond, stat_in.at[other], stat_sem.at[other], {"fsdp": other})
    stat = stat_in[0]
    for j in range(1, groups):
        stat = stat + stat_in[j]
    row_mean = stat[:1] / MODEL_WIDTH
    own = gathered[STASH, z].astype(F32)
    own_gain = gain_columns[pl.ds(pl.multiple_of(z * share, 16), share)]
    d_input = scale_backward * own_gain * d_share - own * scale_backward**3 * row_mean
    input_grad[0] = (gathered[UP, z].astype(F32) + d_input).astype(BF16)
    summed = scatter_total(FWD)
    forward_out[0] = (gathered[ROWS, z].astype(F32) + summed).astype(BF16)
    for cond, copy in pending:
        when(cond, lambda copy=copy: copy.wait_send())


def per_device(*args):
    args = tuple(jnp.swapaxes(arg, -1, -2) for arg in args[:5]) + args[5:]
    embedded = args[0]
    share, length = embedded.shape
    w_query, w_key, w_out = args[6], args[7], args[9]
    sections = lax.axis_size("pipe")
    chips = lax.axis_size("seq") // 2
    groups = lax.axis_size("fsdp")
    hops = min(WINDOW_TOKENS // length, lax.axis_size("seq") - 1)
    reach = min((hops + 1) // 2, chips - 1)
    slots = 2 * (reach + 1)
    width = w_key.shape[2]
    kv_heads = width // HEAD_SIZE
    anywhere = pl.BlockSpec(memory_space=pl.ANY)
    inside = pl.BlockSpec(memory_space=pltpu.VMEM)
    sent = jax.ShapeDtypeStruct((1, share, length), BF16)
    dma = pltpu.SemaphoreType.DMA
    call = pl.pallas_call(
        functools.partial(kernel, (sections, chips, groups, reach)),
        out_shape=(sent, sent),
        in_specs=[anywhere] * 5 + [inside] + [anywhere] * 4 + [inside] * 2,
        out_specs=(inside, inside),
        scratch_shapes=[
            pltpu.VMEM(w_query.shape[1:], BF16),
            pltpu.VMEM(w_key.shape[1:], BF16),
            pltpu.VMEM(w_key.shape[1:], BF16),
            pltpu.VMEM(w_out.shape[1:], BF16),
            pltpu.VMEM((3, groups, share, length), BF16),
            pltpu.VMEM((groups * share, length), F32),
            pltpu.VMEM((2, slots, length, 2 * width), BF16),
            pltpu.VMEM((2, length, w_query.shape[2]), BF16),
            pltpu.VMEM((kv_heads, 2 * length, slots * length), F32),
            pltpu.VMEM((slots, length, 2 * width), F32),
            pltpu.VMEM((reach + 1, length, 2 * width), BF16),
            pltpu.VMEM((reach + 1, length, 2 * width), BF16),
            pltpu.VMEM((max(reach, 1), length, 2 * width), BF16),
            pltpu.VMEM((max(reach, 1), length, 2 * width), BF16),
            pltpu.VMEM((2, groups, share, length), F32),
            pltpu.VMEM((2, 2, groups, share, length), BF16),
            pltpu.VMEM((2, 2, groups, share, length), BF16),
            pltpu.VMEM((8, length), F32),
            pltpu.VMEM((groups, 8, length), F32),
            dma((7,)),
            dma((20 * groups + 12 * (reach + 1),)),
            dma((3, groups)),
            dma((2,)),
            dma((2, slots)),
            dma((reach + 1,)),
            dma((max(reach, 1),)),
            dma((2, 2, groups)),
            dma((groups,)),
        ],
        compiler_params=pltpu.CompilerParams(
            collective_id=0, has_side_effects=True, vmem_limit_bytes=56 * 1024 * 1024
        ),
        cost_estimate=pl.CostEstimate(
            flops=4_000_000_000, bytes_accessed=10_000_000, transcendentals=500_000
        ),
    )
    return tuple(jnp.swapaxes(out, 1, 2) for out in call(*args))


def solution(mesh):
    placed = (
        P("seq", "fsdp"),
        P("pipe", "seq", "fsdp"),
        P("pipe", "seq", "fsdp"),
        P("pipe", "seq", "fsdp"),
        P("seq", "fsdp"),
        P("pipe", None),
        P("pipe", None, "fsdp"),
        P("pipe", None, "fsdp"),
        P("pipe", None, "fsdp"),
        P("pipe", "fsdp", None),
        P("pipe", None),
        P("pipe", None),
    )
    return jax.shard_map(
        per_device,
        mesh=mesh,
        in_specs=placed,
        out_specs=(P("pipe", "seq", "fsdp"), P("pipe", "seq", "fsdp")),
        check_vma=False,
    )
```

```python
import functools

import jax
import jax.numpy as jnp
from jax import lax
from jax.experimental import pallas as pl
from jax.experimental.pallas import tpu as pltpu
from jax.sharding import PartitionSpec as P

MODEL_WIDTH = 2688
HEAD_SIZE = 128
WINDOW_TOKENS = 512
MESH = pl.DeviceIdType.MESH
F32 = jnp.float32
BF16 = jnp.bfloat16
STASH, UP, ROWS = 0, 1, 2
BWD, FWD = 0, 1
PIECES = 2


def nn(left, right):
    return lax.dot_general(left, right, (((1,), (0,)), ((), ())), preferred_element_type=F32)


def nt(left, right):
    return lax.dot_general(left, right, (((1,), (1,)), ((), ())), preferred_element_type=F32)


def tn(left, right):
    return lax.dot_general(left, right, (((0,), (0,)), ((), ())), preferred_element_type=F32)


def kernel(
    sizes,
    embedded,
    sent_forward,
    stashed,
    sent_backward,
    loss_grad,
    gain_ref,
    w_query,
    w_key,
    w_value,
    w_out,
    docs_fwd,
    docs_bwd,
    forward_out,
    input_grad,
    wq,
    wk,
    wv,
    wo,
    gathered,
    gain_columns,
    kv_window,
    q_rows,
    probs,
    terms,
    pair_out,
    pair_in,
    chip_out,
    chip_in,
    part,
    rs_out,
    rs_in,
    stat_in,
    local_sem,
    send_sem,
    gather_sem,
    pipe_sem,
    kv_sem,
    pair_sem,
    chip_sem,
    rs_sem,
    stat_sem,
):
    sections, chips, groups, reach = sizes
    share, length = embedded.shape
    section = lax.axis_index("pipe")
    seq = lax.axis_index("seq")
    z = lax.axis_index("fsdp")
    chip, core = seq // 2, lax.rem(seq, 2)
    sibling = seq + 1 - 2 * core
    slots = 2 * (reach + 1)
    scale = HEAD_SIZE ** (-0.5)
    pending = []

    def when(cond, action):
        pl.when(cond)(action)

    def remote(src, dst, recv, target):
        index = len(pending)
        copy = pltpu.make_async_remote_copy(
            src_ref=src,
            dst_ref=dst,
            send_sem=send_sem.at[index],
            recv_sem=recv,
            device_id=target,
            device_id_type=MESH,
        )
        return copy

    def send(cond, src, dst, recv, target):
        copy = remote(src, dst, recv, target)
        pending.append((cond, copy))
        when(cond, lambda: copy.start())

    def arrive(cond, dst, recv, target):
        copy = pltpu.make_async_remote_copy(
            src_ref=dst,
            dst_ref=dst,
            send_sem=send_sem.at[0],
            recv_sem=recv,
            device_id=target,
            device_id_type=MESH,
        )
        when(cond, lambda: copy.wait_recv())

    def local(src, dst, index):
        return pltpu.make_async_copy(src, dst, local_sem.at[index])

    own_stash = local(stashed.at[0], gathered.at[STASH, z], 0)
    own_up = local(loss_grad, gathered.at[UP, z], 1)
    own_rows = local(embedded, gathered.at[ROWS, z], 2)
    weights = [
        local(w_key.at[0], wk, 3),
        local(w_value.at[0], wv, 4),
        local(w_query.at[0], wq, 5),
        local(w_out.at[0], wo, 6),
    ]
    own_stash.start()
    when(section == sections - 1, lambda: own_up.start())
    when(section == 0, lambda: own_rows.start())
    for copy in weights:
        copy.start()

    barrier = pltpu.get_barrier_semaphore()
    neighbours = [
        (z > 0, {"fsdp": z - 1}),
        (z < groups - 1, {"fsdp": z + 1}),
        (section > 0, {"pipe": section - 1}),
        (section < sections - 1, {"pipe": section + 1}),
        (seq >= 0, {"seq": sibling}),
    ]
    for e in range(1, reach + 1):
        neighbours.append((chip >= e, {"seq": seq - 2 * e}))
        neighbours.append((chip + e < chips, {"seq": seq + 2 * e}))
    for d in range(2, groups):
        neighbours.append((z - d >= 0, {"fsdp": z - d}))
        neighbours.append((z + d < groups, {"fsdp": z + d}))
    total = jnp.int32(0)
    for cond, target in neighbours:
        total = total + cond.astype(jnp.int32)

        def greet(target=target):
            pl.semaphore_signal(barrier, inc=1, device_id=target, device_id_type=MESH)

        when(cond, greet)
    pl.semaphore_wait(barrier, total)

    send(
        section > 0,
        sent_backward.at[0],
        gathered.at[UP, z],
        pipe_sem.at[0],
        {"pipe": section - 1},
    )
    send(
        section < sections - 1,
        sent_forward.at[0],
        gathered.at[ROWS, z],
        pipe_sem.at[1],
        {"pipe": section + 1},
    )

    turn = 1

    def inside_line(*places):
        conds = [(place >= 0) & (place < groups) for place in places]
        return functools.reduce(jnp.logical_and, conds)

    def gather_from(array, distance, source=None):
        for step in (turn, -turn):
            at, target = z - step * distance, z + step
            if distance:
                arrive(
                    inside_line(at),
                    gathered.at[array, at],
                    gather_sem.at[array, at],
                    {"fsdp": z - step},
                )
            send(
                inside_line(at, target),
                gathered.at[array, at] if source is None else source,
                gathered.at[array, at],
                gather_sem.at[array, at],
                {"fsdp": target},
            )

    def whole_rows(array):
        return gathered[array].reshape(groups * share, length)


    def project(array, which):
        rows = whole_rows(array).astype(F32)
        row_scale = lax.rsqrt(jnp.mean(rows * rows, axis=0, keepdims=True) + 1e-06)
        h = jnp.transpose((rows * row_scale * gain_columns[...]).astype(BF16))
        half = wk.shape[1]
        kv_window[which, core, :, :half] = nn(h, wk[...]).astype(BF16)
        kv_window[which, core, :, half:] = nn(h, wv[...]).astype(BF16)
        spread(which)
        q_rows[which] = nn(h, wq[...]).astype(BF16)
        return row_scale

    def spread(which):
        for e in range(1, reach + 1):
            slot = 2 * e + core
            send(
                chip + e < chips,
                kv_window.at[which, core],
                kv_window.at[which, slot],
                kv_sem.at[which, slot],
                {"seq": seq + 2 * e},
            )
        send(
            core == 0,
            kv_window.at[which, core],
            kv_window.at[which, core],
            kv_sem.at[which, core],
            {"seq": sibling},
        )

    def share_pair(which):
        for e in range(1, reach + 1):
            slot = 2 * e + core
            arrive(
                chip >= e, kv_window.at[which, slot], kv_sem.at[which, slot], {"seq": sibling}
            )
            send(
                chip >= e,
                kv_window.at[which, slot],
                kv_window.at[which, slot],
                kv_sem.at[which, slot],
                {"seq": sibling},
            )

    def take_pair(which):
        arrive(core == 1, kv_window.at[which, 0], kv_sem.at[which, 0], {"seq": sibling})
        for e in range(1, reach + 1):
            slot = 2 * e + 1 - core
            arrive(
                chip >= e, kv_window.at[which, slot], kv_sem.at[which, slot], {"seq": sibling}
            )

    def clear_absent():
        for which in (BWD, FWD):

            def clear(slot, which=which):
                kv_window[which, slot] = jnp.zeros(kv_window.shape[2:], BF16)

            when(core == 0, lambda: clear(1))
            for e in range(1, reach + 1):

                def both(e=e):
                    clear(2 * e)
                    clear(2 * e + 1)

                when(chip < e, both)

    def keep_mask(docs):
        start = pl.multiple_of(seq * length, 128)
        own = docs[:, pl.ds(start, length)].astype(F32)
        own_docs = jnp.transpose(jnp.broadcast_to(own, (length, length)))
        q_pos = seq * length + lax.broadcasted_iota(jnp.int32, (length, length), 0)
        pieces = []
        for slot in range(slots):
            first = (2 * (chip - slot // 2) + slot % 2) * length
            at = pl.multiple_of(jnp.maximum(first, 0), 128)
            other = docs[:, pl.ds(at, length)].astype(F32)
            k_pos = first + lax.broadcasted_iota(jnp.int32, (length, length), 1)
            keep = (k_pos >= 0) & (k_pos <= q_pos) & (q_pos - k_pos < WINDOW_TOKENS)
            keep = keep & (own_docs == jnp.broadcast_to(other, (length, length)))
            pieces.append(jnp.where(keep, 0.0, -1e30))
        bias = jnp.concatenate(pieces, axis=1)
        return jnp.concatenate([bias, bias], axis=0)

    def window_part(which, column):
        return jnp.concatenate(
            [
                kv_window[which, slot, :, column * HEAD_SIZE : (column + 1) * HEAD_SIZE]
                for slot in range(slots)
            ],
            axis=0,
        )

    def pair_rows(values, head):
        low = 2 * head * HEAD_SIZE
        return jnp.concatenate(
            [values[:, low : low + HEAD_SIZE], values[:, low + HEAD_SIZE : low + 2 * HEAD_SIZE]],
            axis=0,
        )

    kv_heads = wk.shape[1] // HEAD_SIZE

    def softmax(which, head, bias):
        queries = pair_rows(q_rows[which], head)
        scores = nt(queries, window_part(which, head)) * scale
        scores = jnp.where(bias < 0.0, bias, scores)
        top = jnp.max(scores, axis=-1, keepdims=True)
        expo = jnp.exp(scores - top)
        return expo / jnp.sum(expo, axis=-1, keepdims=True)

    def scatter_from(which, distance):
        for piece in range(PIECES):
            rows = pl.ds(piece * (share // PIECES), share // PIECES)
            for step in (turn, -turn):
                side = (1 - step) // 2
                at = z + step * distance
                cond, more = inside_line(at), inside_line(z - step)
                came = rs_in.at[which, side, at, rows]
                sem = rs_sem.at[which, side, at, piece]
                arrive(cond & more, came, sem, {"fsdp": z + step})

                def added(side=side, at=at, rows=rows):
                    rs_out[which, side, at, rows] = (
                        part[which, at, rows] + rs_in[which, side, at, rows].astype(F32)
                    ).astype(BF16)

                def alone(side=side, at=at, rows=rows):
                    rs_out[which, side, at, rows] = part[which, at, rows].astype(BF16)

                when(cond & more, added)
                when(cond & jnp.logical_not(more), alone)
                send(cond, rs_out.at[which, side, at, rows], came, sem, {"fsdp": z + step})

    def scatter_total(which):
        for piece in range(PIECES):
            rows = pl.ds(piece * (share // PIECES), share // PIECES)
            for side, more, source in (
                (0, z > 0, {"fsdp": z - 1}),
                (1, z < groups - 1, {"fsdp": z + 1}),
            ):
                came = rs_in.at[which, side, z, rows]
                arrive(more, came, rs_sem.at[which, side, z, piece], source)

                def add(side=side, rows=rows):
                    part[which, z, rows] = part[which, z, rows] + rs_in[
                        which, side, z, rows
                    ].astype(F32)

                when(more, add)
        return part[which, z]

    def split_part(which, values):
        part[which] = values.reshape(groups, share, length)

    gather_from(STASH, 0, stashed.at[0])
    when(section == sections - 1, lambda: own_up.wait())
    arrive(section < sections - 1, gathered.at[UP, z], pipe_sem.at[0], {"pipe": section})
    gather_from(UP, 0)
    clear_absent()
    for low in range(0, groups * share, length):
        row = jnp.broadcast_to(gain_ref[:, low : low + length], (length, length))
        gain_columns[low : low + length] = jnp.transpose(row)
    own_stash.wait()
    for d in range(1, groups):
        gather_from(STASH, d)
    gather_from(UP, 1)
    when(section == 0, lambda: own_rows.wait())
    arrive(section > 0, gathered.at[ROWS, z], pipe_sem.at[1], {"pipe": section})
    gather_from(ROWS, 0)
    for copy in weights[:3]:
        copy.wait()

    scale_backward = project(STASH, BWD)
    gather_from(UP, 2) if groups > 2 else None
    share_pair(BWD)
    bias = keep_mask(docs_bwd)
    take_pair(BWD)
    for head in range(kv_heads):
        probs[head] = softmax(BWD, head, bias)
    for d in range(3, groups):
        gather_from(UP, d)
    gather_from(ROWS, 1)
    weights[3].wait()
    d_attn = jnp.transpose(nn(wo[...], whole_rows(UP)).astype(BF16))
    dq_parts = []
    for head in range(kv_heads):
        p = probs[head]
        gradient = pair_rows(d_attn, head)
        keys = window_part(BWD, head)
        dp = nt(gradient, window_part(BWD, kv_heads + head))
        delta = jnp.sum(p * dp, axis=-1, keepdims=True)
        ds = (p * (dp - delta)).astype(BF16)
        dk = tn(ds, pair_rows(q_rows[BWD], head)) * scale
        dv = tn(p.astype(BF16), gradient)
        for slot in range(slots):
            low = head * HEAD_SIZE
            rows = slice(slot * length, (slot + 1) * length)
            terms[slot, :, low : low + HEAD_SIZE] = dk[rows]
            low = low + kv_heads * HEAD_SIZE
            terms[slot, :, low : low + HEAD_SIZE] = dv[rows]
        dq = (nn(ds, keys) * scale).astype(BF16)
        dq_parts += [dq[:length], dq[length:]]
    for e in list(range(1, reach + 1)) + [0]:
        cond = (chip >= e) if e else (core == 1)

        def stage(e=e):
            pair_out[e] = terms[2 * e + 1 - core].astype(BF16)

        when(cond, stage)
        send(cond, pair_out.at[e], pair_in.at[e], pair_sem.at[e], {"seq": sibling})
    for e in range(1, reach + 1):
        arrive(chip >= e, pair_in.at[e], pair_sem.at[e], {"seq": sibling})

        def stage(e=e):
            chip_out[e - 1] = (terms[2 * e + core] + pair_in[e].astype(F32)).astype(BF16)

        when(chip >= e, stage)
        send(
            chip >= e,
            chip_out.at[e - 1],
            chip_in.at[e - 1],
            chip_sem.at[e - 1],
            {"seq": seq - 2 * e},
        )
    gather_from(ROWS, 2) if groups > 2 else None
    dq_local = jnp.concatenate(dq_parts, axis=1)
    d_norm = nt(wq[...], dq_local)
    arrive(core == 0, pair_in.at[0], pair_sem.at[0], {"seq": sibling})

    def add_pair():
        terms[core] = terms[core] + pair_in[0].astype(F32)

    when(core == 0, add_pair)
    for e in range(1, reach + 1):
        arrive(chip + e < chips, chip_in.at[e - 1], chip_sem.at[e - 1], {"seq": sibling})

        def add_chip(e=e):
            terms[core] = terms[core] + chip_in[e - 1].astype(F32)

        when(chip + e < chips, add_chip)
    owned = terms[core].astype(BF16)
    half = wk.shape[1]
    d_norm = d_norm + nt(wk[...], owned[:, :half]) + nt(wv[...], owned[:, half:])
    split_part(BWD, d_norm)
    for d in range(groups - 1, 0, -1):
        if d == 1:
            for far in range(3, groups):
                gather_from(ROWS, far)
        scatter_from(BWD, d)
    rows = whole_rows(STASH).astype(F32)
    row_part = jnp.sum(rows * gain_columns[...] * d_norm, axis=0, keepdims=True)
    stat_in[z] = jnp.broadcast_to(row_part, (8, length))
    for d in range(1, groups):
        for cond, other in ((z + d < groups, z + d), (z - d >= 0, z - d)):
            send(cond, stat_in.at[z], stat_in.at[z], stat_sem.at[z], {"fsdp": other})

    project(ROWS, FWD)
    share_pair(FWD)
    bias = keep_mask(docs_fwd)
    take_pair(FWD)
    attn_parts = []
    for head in range(kv_heads):
        p = softmax(FWD, head, bias).astype(BF16)
        attn = nn(p, window_part(FWD, kv_heads + head)).astype(BF16)
        attn_parts += [attn[:length], attn[length:]]
    split_part(FWD, jnp.transpose(nn(jnp.concatenate(attn_parts, axis=1), wo[...])))
    for d in range(groups - 1, 0, -1):
        scatter_from(FWD, d)

    d_share = scatter_total(BWD)
    for d in range(1, groups):
        for cond, other in ((z + d < groups, z + d), (z - d >= 0, z - d)):
            arrive(cond, stat_in.at[other], stat_sem.at[other], {"fsdp": other})
    stat = stat_in[0]
    for j in range(1, groups):
        stat = stat + stat_in[j]
    row_mean = stat[:1] / MODEL_WIDTH
    own = gathered[STASH, z].astype(F32)
    own_gain = gain_columns[pl.ds(pl.multiple_of(z * share, 16), share)]
    d_input = scale_backward * own_gain * d_share - own * scale_backward**3 * row_mean
    input_grad[0] = (gathered[UP, z].astype(F32) + d_input).astype(BF16)
    summed = scatter_total(FWD)
    forward_out[0] = (gathered[ROWS, z].astype(F32) + summed).astype(BF16)
    for cond, copy in pending:
        when(cond, lambda copy=copy: copy.wait_send())


def per_device(*args):
    args = tuple(jnp.swapaxes(arg, -1, -2) for arg in args[:5]) + args[5:]
    embedded = args[0]
    share, length = embedded.shape
    w_query, w_key, w_out = args[6], args[7], args[9]
    sections = lax.axis_size("pipe")
    chips = lax.axis_size("seq") // 2
    groups = lax.axis_size("fsdp")
    hops = min(WINDOW_TOKENS // length, lax.axis_size("seq") - 1)
    reach = min((hops + 1) // 2, chips - 1)
    slots = 2 * (reach + 1)
    width = w_key.shape[2]
    kv_heads = width // HEAD_SIZE
    anywhere = pl.BlockSpec(memory_space=pl.ANY)
    inside = pl.BlockSpec(memory_space=pltpu.VMEM)
    sent = jax.ShapeDtypeStruct((1, share, length), BF16)
    dma = pltpu.SemaphoreType.DMA
    call = pl.pallas_call(
        functools.partial(kernel, (sections, chips, groups, reach)),
        out_shape=(sent, sent),
        in_specs=[anywhere] * 5 + [inside] + [anywhere] * 4 + [inside] * 2,
        out_specs=(inside, inside),
        scratch_shapes=[
            pltpu.VMEM(w_query.shape[1:], BF16),
            pltpu.VMEM(w_key.shape[1:], BF16),
            pltpu.VMEM(w_key.shape[1:], BF16),
            pltpu.VMEM(w_out.shape[1:], BF16),
            pltpu.VMEM((3, groups, share, length), BF16),
            pltpu.VMEM((groups * share, length), F32),
            pltpu.VMEM((2, slots, length, 2 * width), BF16),
            pltpu.VMEM((2, length, w_query.shape[2]), BF16),
            pltpu.VMEM((kv_heads, 2 * length, slots * length), F32),
            pltpu.VMEM((slots, length, 2 * width), F32),
            pltpu.VMEM((reach + 1, length, 2 * width), BF16),
            pltpu.VMEM((reach + 1, length, 2 * width), BF16),
            pltpu.VMEM((max(reach, 1), length, 2 * width), BF16),
            pltpu.VMEM((max(reach, 1), length, 2 * width), BF16),
            pltpu.VMEM((2, groups, share, length), F32),
            pltpu.VMEM((2, 2, groups, share, length), BF16),
            pltpu.VMEM((2, 2, groups, share, length), BF16),
            pltpu.VMEM((groups, 8, length), F32),
            dma((7,)),
            dma(((12 + 4 * PIECES) * groups + 12 * (reach + 1),)),
            dma((3, groups)),
            dma((2,)),
            dma((2, slots)),
            dma((reach + 1,)),
            dma((max(reach, 1),)),
            dma((2, 2, groups, PIECES)),
            dma((groups,)),
        ],
        compiler_params=pltpu.CompilerParams(
            collective_id=0, has_side_effects=True, vmem_limit_bytes=56 * 1024 * 1024
        ),
        cost_estimate=pl.CostEstimate(
            flops=4_000_000_000, bytes_accessed=10_000_000, transcendentals=500_000
        ),
    )
    return tuple(jnp.swapaxes(out, 1, 2) for out in call(*args))


def solution(mesh):
    placed = (
        P("seq", "fsdp"),
        P("pipe", "seq", "fsdp"),
        P("pipe", "seq", "fsdp"),
        P("pipe", "seq", "fsdp"),
        P("seq", "fsdp"),
        P("pipe", None),
        P("pipe", None, "fsdp"),
        P("pipe", None, "fsdp"),
        P("pipe", None, "fsdp"),
        P("pipe", "fsdp", None),
        P("pipe", None),
        P("pipe", None),
    )
    return jax.shard_map(
        per_device,
        mesh=mesh,
        in_specs=placed,
        out_specs=(P("pipe", "seq", "fsdp"), P("pipe", "seq", "fsdp")),
        check_vma=False,
    )
```
